256 devices in a mesh: ctx: 32 (over z, x), head: 8 (over y, core).
Axes of the slice: x: 4, y: 4, z: 8, core: 2. Of those that a mesh axis runs over, the one named last changes fastest.
Arguments:
- tokens: bfloat16 [32768, 2048], P(('ctx', 'head')), may hold values from -6 to 6
- projection: bfloat16 [2048, 4096], P(None, 'head'), may hold values from -0.125 to 0.125
- context_state: float32 [16, 2080, 64], P('head'), may hold values from -24 to 24
- norm_gain: float32 [2048], P('head'), may hold values from 0.1 to 1.9
Outputs:
- retained: bfloat16 [32768, 2048], P(('ctx', 'head'))
The draws below stay inside these ranges and needn't reach their ends.
All inputs are finite; a program needn't handle non-finite values.
Results may differ from the reference program's by a relative error of at most 0.008.
Values may be sent and summed in bfloat16 or wider, within the bound.
A program may use at most 192 MiB of HBM per device.

```python
import math
import jax
import jax.numpy as jnp
import numpy as np
from jax import lax

D = 2048
QUERY_HEADS = 32
KEY_HEADS = 16
HEAD_WIDTH = 64
TOK_DEV = 1024
PAIR_FEATURES = 2080
BLOCKS = 32
TOKENS = 32768
PROJ = 4096


def level_of(key, dims, pieces, smallest, high):
    gain, own = 1.0, jax.random.fold_in(key, 6)
    for position, blocks in pieces:
        heights = jnp.exp(jax.random.uniform(jax.random.fold_in(own, position), (blocks,), jnp.float32, smallest / len(pieces), high / len(pieces)))
        gain = gain * jnp.repeat(heights, dims[position] // blocks).reshape([-1 if axis == position else 1 for axis in range(len(dims))])
    return gain


def noise(stream_key, dims, scale, bound, shards=(), held_as=jnp.bfloat16):
    values = jax.random.normal(stream_key, dims, jnp.float32) * scale
    if len(shards) > 0:
        values = level_of(stream_key, dims, shards, -0.22, 0.18) * values
    return jnp.clip(values, min=-bound, max=bound).astype(held_as)


def setup_inputs(seed: int = 0) -> dict:
    seeds = jax.random.split(jax.random.key(seed), 5)
    tokens = noise(seeds[0], (TOKENS, D), 1.0, 6.0, ((0, 256),))
    projection = noise(seeds[1], (D, PROJ), D ** -0.5, 0.125, ((1, 8),))
    context_state = noise(seeds[2], (KEY_HEADS, PAIR_FEATURES, HEAD_WIDTH), 4.0, 24.0, ((0, 8),), jnp.float32)
    norm_gain = jnp.clip(1.0 + 0.18 * jax.random.normal(seeds[3], (QUERY_HEADS * HEAD_WIDTH,), jnp.float32), 0.1, 1.9)
    return {"tokens": tokens, "projection": projection, "context_state": context_state, "norm_gain": norm_gain}


def pair_tables(size):
    first_index, second_index = np.triu_indices(size)
    pair_weight = np.where(first_index == second_index, 1.0, math.sqrt(2.0)) / math.sqrt(size)
    return (first_index, second_index, pair_weight)

def features(vectors):
    first_index, second_index, pair_weight = pair_tables(vectors.shape[-1])
    return vectors[..., first_index] * vectors[..., second_index] * jnp.asarray(pair_weight, jnp.float32)

def reference(tokens, projection, context_state, norm_gain):
    group_total = QUERY_HEADS // KEY_HEADS
    group_width = (group_total + 2) * HEAD_WIDTH
    causal = jnp.arange(TOK_DEV)[None, :] <= jnp.arange(TOK_DEV)[:, None]

    def single_group(group_index):
        columns = lax.dynamic_slice_in_dim(projection, group_index * group_width, group_width, 1)
        projected = jnp.dot(tokens, columns, preferred_element_type=jnp.float32).astype(jnp.bfloat16)
        blocks = projected.reshape(BLOCKS, TOK_DEV, group_total + 2, HEAD_WIDTH).astype(jnp.float32)
        queries = blocks[:, :, :group_total]
        key_rows = blocks[:, :, group_total]
        values = blocks[:, :, group_total + 1]

        def state_of(key_pair):
            block_keys, block_values = key_pair
            expanded = features(block_keys).astype(jnp.bfloat16)
            return jnp.dot(expanded.T, block_values.astype(jnp.bfloat16), preferred_element_type=jnp.float32)
        states = lax.map(state_of, (key_rows, values))
        running = jnp.cumsum(states, axis=0)
        earlier_sum = jnp.concatenate([jnp.zeros((1, PAIR_FEATURES, HEAD_WIDTH), jnp.float32), running[:-1]], axis=0)
        prefix = (context_state[group_index][None] + earlier_sum).astype(jnp.bfloat16)

        def output_of(block_parts):
            query_rows, block_keys, block_values, block_prefix = block_parts
            expanded = features(query_rows).astype(jnp.bfloat16)
            carried_part = jnp.einsum('lgf,fd->lgd', expanded.astype(jnp.float32), block_prefix.astype(jnp.float32))
            scores = jnp.einsum('lgd,md->glm', query_rows, block_keys)
            scores = jnp.where(causal[None], scores * scores / HEAD_WIDTH, 0.0).astype(jnp.bfloat16)
            within = jnp.einsum('glm,md->lgd', scores.astype(jnp.float32), block_values)
            combined = carried_part + within
            inverse_rms = lax.rsqrt(lax.optimization_barrier(jnp.mean(combined * combined, -1, keepdims=True)) + 1e-05)
            return combined * inverse_rms
        normed = lax.map(output_of, (queries, key_rows, values, prefix))
        return normed.reshape(TOKENS, group_total, HEAD_WIDTH)
    head_row_list = lax.map(single_group, jnp.arange(KEY_HEADS))
    gathered = jnp.transpose(head_row_list, (1, 0, 2, 3)).reshape(TOKENS, QUERY_HEADS * HEAD_WIDTH)
    return (gathered * norm_gain[None]).astype(jnp.bfloat16)
```

```python
import math

import jax
import jax.numpy as jnp
from jax import lax
from jax.experimental import pallas as pl
from jax.experimental.pallas import tpu as pltpu
from jax.sharding import PartitionSpec as P

MESH = pl.DeviceIdType.MESH
NZ, NX, NY = 8, 4, 4
WIDTH = 64
TOKENS = 1024
GROUP = 256
DEPTH = 2048
CHUNKS = 17
FEAT = 128 * CHUNKS
PIECE = 384
F32, BF16 = jnp.float32, jnp.bfloat16


def lanes(rows):
    return lax.broadcasted_iota(jnp.int32, (rows, 128), 1)


def left(value, amount):
    return pltpu.roll(value, 128 - amount, 1)


def write_features(twice, store):
    base = jnp.where(lanes(twice.shape[0]) < WIDTH, twice, left(twice, 16))
    for m in range(16):
        store(m, (base * left(twice, 17 + m)).astype(BF16))
    store(16, (twice * twice).astype(BF16))


def doubled(pair, half):
    low = lanes(pair.shape[0]) < WIDTH
    turned = pltpu.roll(pair, WIDTH, 1)
    return jnp.where(low, pair, turned) if half == 0 else jnp.where(low, turned, pair)


def kernel(tok_ref, w_hbm, ctx_hbm, gain_ref, out_ref,
           w_v, ctx_v, xall, q_v, kz_v, vk_v, phik, state, phiq, comb,
           square, ctx_f, ctx_t, xs, xr, zs, zr, es, er, ps, pt, ob,
           local_sem, gs, gr, xs_sem, xr_sem, zs_sem, zr_sem, es_sem, er_sem, ps_sem, pr_sem, os_sem, or_sem):
    me_ctx, me_head = lax.axis_index("ctx"), lax.axis_index("head")
    z, x = me_ctx // NX, me_ctx % NX
    y, core = me_head // 2, me_head % 2
    up, down, far = (y + 1) % NY, (y + NY - 1) % NY, (y + 2) % NY

    def head_partner(k):
        return (me_head + k) % (2 * NY)

    barrier = pltpu.get_barrier_semaphore()
    for k in range(1, 2 * NY):
        pl.semaphore_signal(barrier, inc=1, device_id=(me_ctx, head_partner(k)), device_id_type=MESH)
    for k in range(1, NX):
        pl.semaphore_signal(barrier, inc=1, device_id=(z * NX + (x + k) % NX, me_head), device_id_type=MESH)
    for k in range(1, NZ):
        pl.semaphore_signal(barrier, inc=1, device_id=(((z + k) % NZ) * NX + x, me_head), device_id_type=MESH)

    own = pltpu.make_async_copy(tok_ref, xall.at[me_head], local_sem.at[0])
    weights = pltpu.make_async_copy(w_hbm, w_v, local_sem.at[1])
    context = pltpu.make_async_copy(ctx_hbm, ctx_v, local_sem.at[2])
    own.start()
    weights.start()
    context.start()
    pl.semaphore_wait(barrier, 2 * NY - 1 + NX - 1 + NZ - 1)

    sent = []

    def send(src, dst, send_sem, recv_sem, device):
        copy = pltpu.make_async_remote_copy(
            src_ref=src, dst_ref=dst, send_sem=send_sem, recv_sem=recv_sem, device_id=device, device_id_type=MESH)
        copy.start()
        sent.append(copy)

    def arrived(dst, send_sem, recv_sem):
        pltpu.make_async_remote_copy(
            src_ref=dst, dst_ref=dst, send_sem=send_sem, recv_sem=recv_sem,
            device_id=(me_ctx, head_partner(1)), device_id_type=MESH).wait_recv()

    low, high = pl.ds(0, 64), pl.ds(64, 64)
    sib = (me_ctx, y * 2 + 1 - core)
    to_up, to_down = (me_ctx, up * 2 + core), (me_ctx, down * 2 + core)
    h_up, h_down, h_far = up * 2 + core, down * 2 + core, far * 2 + core
    s_up, s_down, s_far = up * 2 + 1 - core, down * 2 + 1 - core, far * 2 + 1 - core

    send(tok_ref.at[low], xall.at[me_head, low], gs.at[1], gr.at[1], to_up)
    send(tok_ref.at[high], xall.at[me_head, high], gs.at[2], gr.at[2], to_down)
    send(tok_ref, xall.at[me_head], gs.at[0], gr.at[0], sib)
    send(tok_ref.at[high], xall.at[me_head, high], gs.at[3], gr.at[3], to_up)
    send(tok_ref.at[low], xall.at[me_head, low], gs.at[4], gr.at[4], to_down)

    def pass_on(row, half, slot, device):
        send(xall.at[row, half], xall.at[row, half], gs.at[slot], gr.at[slot], device)

    def have(row, half, slot):
        arrived(xall.at[row, half], gs.at[slot], gr.at[slot])

    def project(group, first):
        rows = xall[pl.ds(2 * group, 2)].reshape(GROUP, DEPTH)
        made = jnp.dot(rows, w_v[...], preferred_element_type=F32).astype(BF16)
        for h in range(2):
            q_v[h, group] = made[:, 256 * h:256 * h + 128]
            pair = made[:, 256 * h + 128:256 * h + 256].astype(F32)
            kz_v[h, group] = jnp.where(lanes(GROUP) < WIDTH, pair, 0.0).astype(BF16)
            vk_v[h, group] = pltpu.roll(pair, WIDTH, 1).astype(BF16)
            twice = doubled(pair, 0)

            def store(m, value):
                phik[:, 128 * m:128 * m + 128] = value

            write_features(twice, store)
            values = pair.T[WIDTH:].astype(BF16)
            update = jnp.dot(values, phik[...], preferred_element_type=F32)
            if first:
                state[h] = update
            else:
                state[h] += update

    own.wait()
    weights.wait()
    arrived(xall.at[me_head], gs.at[0], gr.at[0])
    project(y, True)

    have(h_down, low, 1)
    pass_on(h_down, low, 5, to_up)
    pass_on(h_down, low, 7, sib)
    have(h_up, high, 2)
    pass_on(h_up, high, 6, to_down)
    pass_on(h_up, high, 8, sib)

    context.wait()
    start = 0
    for i in range(WIDTH):
        count = min(40, WIDTH - i)
        both = jnp.concatenate([ctx_v[0, start:start + count], ctx_v[1, start:start + count]], axis=1)
        square[129 * i:129 * i + count] = both
        start += WIDTH - i
    start = 0
    for i in range(WIDTH // 2):
        count = WIDTH // 2 - i
        both = jnp.concatenate(
            [ctx_v[0, start + 32:start + 32 + count], ctx_v[1, start + 32:start + 32 + count]], axis=1)
        square[pl.ds(128 * (i + 32) + 64 + i, count, 128)] = both
        start += WIDTH - i
    for apart in range(33):
        rows = square[pl.ds(apart, WIDTH, 129)]
        if apart == 0:
            ctx_f[2048:2112] = rows
            ctx_f[2112:2176] = jnp.zeros_like(rows)
        elif apart > 16:
            ctx_f[128 * (apart - 17):128 * (apart - 17) + 64] = rows
        else:
            at = 128 * (apart - 1) + 64
            ctx_f[at:at + 48] = rows[16:]
            ctx_f[at + 48:at + 64] = rows[:16]
    feature = lax.broadcasted_iota(jnp.int32, (1, FEAT), 1)
    in_second = (feature % 128) >= WIDTH
    diagonal = (feature >= 2048) & (feature < 2112)
    unused = feature >= 2112
    twin = (feature >= 15 * 128) & (feature < 15 * 128 + 64)
    square_weight = jnp.where(unused, 0.0, jnp.where(diagonal | twin, 1.0 / 64, 2.0 / 64)).astype(F32)
    single_weight = jnp.where(
        unused, 0.0, jnp.where(diagonal, 1.0 / 8, jnp.where(twin, math.sqrt(2.0) / 16, math.sqrt(2.0) / 8))).astype(F32)
    for m in range(CHUNKS):
        turned = ctx_f[128 * m:128 * m + 128].T
        ctx_t[:, :, 128 * m:128 * m + 128] = turned.reshape(8, 16, 128)

    have(h_down, high, 3)
    pass_on(h_down, high, 9, sib)
    have(h_up, low, 4)
    pass_on(h_up, low, 10, sib)
    have(s_down, low, 7)
    have(s_down, high, 9)
    project(down, False)
    have(s_up, high, 8)
    have(s_up, low, 10)
    project(up, False)
    have(h_far, low, 5)
    pass_on(h_far, low, 11, sib)
    have(h_far, high, 6)
    pass_on(h_far, high, 12, sib)
    have(s_far, low, 11)
    have(s_far, high, 12)
    project(far, False)

    def x_out(h):
        xs[h] = state[h].reshape(NX, 16, FEAT).astype(BF16)
        xr[h, x] = xs[h, x]
        for k in range(1, NX):
            there = (x + k) % NX
            send(xs.at[h, there], xr.at[h, x], xs_sem.at[h, k], xr_sem.at[h, k], (z * NX + there, me_head))

    def x_in(h):
        for k in range(1, NX):
            arrived(xr.at[h, (x + NX - k) % NX], xs_sem.at[h, k], xr_sem.at[h, k])
        total = xr[h, 0].astype(F32)
        for k in range(1, NX):
            total += xr[h, k].astype(F32)
        total = total.astype(BF16)
        for k in range(NZ):
            zs[h, k] = total[:, 256 * k:256 * k + PIECE]
        zr[h, z] = zs[h, z]
        for k in range(1, NZ):
            there = (z + k) % NZ
            send(zs.at[h, there], zr.at[h, z], zs_sem.at[h, k], zr_sem.at[h, k], (there * NX + x, me_head))

    def z_in(h):
        for k in range(1, NZ):
            arrived(zr.at[h, (z + NZ - k) % NZ], zs_sem.at[h, k], zr_sem.at[h, k])
        running = jnp.zeros((16, PIECE), F32)
        for k in range(NZ):
            es[h, k] = running.astype(BF16)
            running += zr[h, k].astype(F32)
        er[h, z] = es[h, z]
        for k in range(1, NZ):
            there = (z + k) % NZ
            send(es.at[h, there], er.at[h, z], es_sem.at[h, k], er_sem.at[h, k], (there * NX + x, me_head))

    def e_in(h):
        for k in range(1, NZ):
            arrived(er.at[h, (z + NZ - k) % NZ], es_sem.at[h, k], er_sem.at[h, k])
        earlier = jnp.concatenate(
            [er[h, k, :, :256] for k in range(NZ - 1)] + [er[h, NZ - 1]], axis=1).astype(F32)
        before = ctx_t[4 * h + x] * single_weight
        running = earlier
        for k in range(NX):
            ps[h, k] = (before + running * square_weight).astype(BF16)
            if k < NX - 1:
                running += xr[h, k].astype(F32)
        pt[h, x] = ps[h, x]
        for k in range(1, NX):
            there = (x + k) % NX
            send(ps.at[h, there], pt.at[h, x], ps_sem.at[h, k], pr_sem.at[h, k], (z * NX + there, me_head))

    causal = (lax.broadcasted_iota(jnp.int32, (GROUP, GROUP), 1)
              <= lax.broadcasted_iota(jnp.int32, (GROUP, GROUP), 0))

    def tile(h, i):
        pair = q_v[h, i].astype(F32)
        for g in range(2):
            twice = doubled(pair, g)

            def store(m, value):
                phiq[h, i, g, :, 128 * m:128 * m + 128] = value

            write_features(twice, store)
            query = twice.astype(BF16)
            total = None
            for j in range(i + 1):
                score = lax.dot_general(
                    query, kz_v[h, j], (((1,), (1,)), ((), ())), preferred_element_type=F32)
                score = score * score * (1.0 / WIDTH)
                if j == i:
                    score = jnp.where(causal, score, 0.0)
                part = jnp.dot(score.astype(BF16), vk_v[h, j], preferred_element_type=F32)
                total = part if total is None else total + part
            comb[h, i, g] = total

    def finish(h):
        for k in range(1, NX):
            arrived(pt.at[h, (x + NX - k) % NX], ps_sem.at[h, k], pr_sem.at[h, k])
        prefix = pt[h].reshape(WIDTH, FEAT)

        def one(i, carry):
            made = []
            for g in range(2):
                carried = lax.dot_general(
                    phiq[h, i, g], prefix, (((1,), (1,)), ((), ())), preferred_element_type=F32)
                combined = carried + comb[h, i, g][:, :WIDTH]
                inverse = lax.rsqrt(jnp.mean(combined * combined, -1, keepdims=True) + 1e-05)
                made.append(combined * inverse)
            both = jnp.concatenate(made, axis=1) * gain_ref[:, 128 * h:128 * h + 128]
            ob[h, pl.ds(2 * i, 2)] = both.astype(BF16).reshape(2, 128, 128)
            return carry

        lax.fori_loop(0, TOKENS // GROUP, one, 0)
        place = pl.ds(pl.multiple_of(me_head * 256 + 128 * h, 128), 128)
        for k in range(1, 2 * NY):
            there = head_partner(k)
            send(ob.at[h, there], out_ref.at[:, place], os_sem.at[h, k], or_sem.at[h, k], (me_ctx, there))
        return pltpu.make_async_copy(ob.at[h, me_head], out_ref.at[:, place], local_sem.at[3 + h])

    x_out(0)
    x_out(1)
    tile(0, 0)
    tile(0, 1)
    tile(0, 2)
    x_in(0)
    tile(0, 3)
    x_in(1)
    tile(1, 0)
    tile(1, 1)
    z_in(0)
    tile(1, 2)
    z_in(1)
    tile(1, 3)
    e_in(0)
    e_in(1)
    last = []
    for h in range(2):
        copy = finish(h)
        copy.start()
        last.append(copy)
    for copy in last:
        copy.wait()
    for h in range(2):
        for k in range(1, 2 * NY):
            there = (me_head + 2 * NY - k) % (2 * NY)
            place = pl.ds(pl.multiple_of(there * 256 + 128 * h, 128), 128)
            arrived(out_ref.at[:, place], os_sem.at[h, k], or_sem.at[h, k])
    for copy in sent:
        copy.wait_send()


def local(tokens, projection, context_state, norm_gain):
    dma = pltpu.SemaphoreType.DMA
    return pl.pallas_call(
        kernel,
        out_shape=jax.ShapeDtypeStruct((128, 2048), BF16),
        in_specs=[pl.BlockSpec(memory_space=pl.ANY)] * 3 + [pl.BlockSpec(memory_space=pltpu.VMEM)],
        out_specs=pl.BlockSpec(memory_space=pl.ANY),
        scratch_shapes=[
            pltpu.VMEM((DEPTH, 512), BF16),
            pltpu.VMEM((2, 2080, WIDTH), F32),
            pltpu.VMEM((2 * NY, 128, DEPTH), BF16),
            pltpu.VMEM((2, 4, GROUP, 128), BF16),
            pltpu.VMEM((2, 4, GROUP, 128), BF16),
            pltpu.VMEM((2, 4, GROUP, 128), BF16),
            pltpu.VMEM((GROUP, FEAT), BF16),
            pltpu.VMEM((2, WIDTH, FEAT), F32),
            pltpu.VMEM((2, 4, 2, GROUP, FEAT), BF16),
            pltpu.VMEM((2, 4, 2, GROUP, 128), F32),
            pltpu.VMEM((64 * 129 + 8, 128), F32),
            pltpu.VMEM((FEAT, 128), F32),
            pltpu.VMEM((8, 16, FEAT), F32),
            pltpu.VMEM((2, NX, 16, FEAT), BF16),
            pltpu.VMEM((2, NX, 16, FEAT), BF16),
            pltpu.VMEM((2, NZ, 16, PIECE), BF16),
            pltpu.VMEM((2, NZ, 16, PIECE), BF16),
            pltpu.VMEM((2, NZ, 16, PIECE), BF16),
            pltpu.VMEM((2, NZ, 16, PIECE), BF16),
            pltpu.VMEM((2, NX, 16, FEAT), BF16),
            pltpu.VMEM((2, NX, 16, FEAT), BF16),
            pltpu.VMEM((2, 2 * NY, 128, 128), BF16),
            dma((5,)),
            dma((13,)),
            dma((13,)),
            dma((2, NX)),
            dma((2, NX)),
            dma((2, NZ)),
            dma((2, NZ)),
            dma((2, NZ)),
            dma((2, NZ)),
            dma((2, NX)),
            dma((2, NX)),
            dma((2, 2 * NY)),
            dma((2, 2 * NY)),
        ],
        compiler_params=pltpu.CompilerParams(
            collective_id=0, has_side_effects=True, vmem_limit_bytes=58 * 2**20),
        cost_estimate=pl.CostEstimate(flops=10 * 10**9, bytes_accessed=8 * 2**20, transcendentals=0),
    )(tokens, projection, context_state, norm_gain.reshape(1, -1))


def solution(mesh):
    placed = (P(("ctx", "head"), None), P(None, "head"), P("head", None, None), P("head"))
    return jax.shard_map(
        local, mesh=mesh, in_specs=placed, out_specs=P(("ctx", "head"), None), check_vma=False
    )
```

```python
import functools
import math

import jax
import jax.numpy as jnp
from jax import lax
from jax.experimental import pallas as pl
from jax.experimental.pallas import tpu as pltpu
from jax.sharding import PartitionSpec as P

MESH = pl.DeviceIdType.MESH
NZ, NX, NY = 8, 4, 4
WIDTH = 64
TOKENS = 1024
GROUP = 256
DEPTH = 2048
CHUNKS = 17
FEAT = 128 * CHUNKS
PAIRS = 2080
PIECE = 384
F32, BF16 = jnp.float32, jnp.bfloat16


def lanes(rows):
    return lax.broadcasted_iota(jnp.int32, (rows, 128), 1)


def left(value, amount):
    return pltpu.roll(value, 128 - amount, 1)


def write_features(twice, store):
    base = jnp.where(lanes(twice.shape[0]) < WIDTH, twice, left(twice, 16))
    for m in range(16):
        store(m, (base * left(twice, 17 + m)).astype(BF16))
    store(16, (twice * twice).astype(BF16))


def doubled(pair, half):
    low = lanes(pair.shape[0]) < WIDTH
    turned = pltpu.roll(pair, WIDTH, 1)
    return jnp.where(low, pair, turned) if half == 0 else jnp.where(low, turned, pair)


def kernel(tok_ref, w_hbm, ctx_hbm, gain_ref, out_ref,
           w_v, ctx_v, xall, q_v, kz_v, vk_v, kv_v, phik, state, phiq, comb,
           square, ctx_f, ctx_t, xs, xr, zs, zr, es, er, tails, ps, pt, turned, ob,
           met, local_sem, gs, gr, xs_sem, xr_sem, zs_sem, zr_sem, es_sem, er_sem, ps_sem, pr_sem, os_sem, or_sem):
    me_ctx, me_head = lax.axis_index("ctx"), lax.axis_index("head")
    z, x = me_ctx // NX, me_ctx % NX
    y, core = me_head // 2, me_head % 2
    up, down, far = (y + 1) % NY, (y + NY - 1) % NY, (y + 2) % NY

    def head_partner(k):
        return (me_head + k) % (2 * NY)

    barrier = pltpu.get_barrier_semaphore()
    sib = (me_ctx, y * 2 + 1 - core)
    for other in (up, down):
        pl.semaphore_signal(barrier, inc=1, device_id=(me_ctx, other * 2), device_id_type=MESH)

    @pl.when(core == 1)
    def _():
        pl.semaphore_signal(barrier, inc=1, device_id=sib, device_id_type=MESH)

    for k in range(1, NX):
        pl.semaphore_signal(barrier, inc=1, device_id=(z * NX + (x + k) % NX, y * 2 + 1), device_id_type=MESH)
    for k in range(1, NZ):
        pl.semaphore_signal(barrier, inc=1, device_id=(((z + k) % NZ) * NX + x, y * 2 + 1), device_id_type=MESH)

    own = pltpu.make_async_copy(tok_ref, xall.at[me_head], local_sem.at[0])
    weights = []
    for n, at in enumerate((128, 384, 0, 256)):
        weights.append(pltpu.make_async_copy(
            w_hbm.at[:, at:at + 128], w_v.at[n // 2, :, 128 * (n % 2):128 * (n % 2) + 128], local_sem.at[5 + n]))
    context = pltpu.make_async_copy(ctx_hbm, ctx_v, local_sem.at[2])
    own.start()
    for part in weights:
        part.start()
    context.start()

    @pl.when(core == 0)
    def _():
        pl.semaphore_wait(barrier, 5)
        pl.semaphore_signal(met.at[0], inc=1, device_id=sib, device_id_type=MESH)

    @pl.when(core == 1)
    def _():
        pl.semaphore_wait(met.at[0], 1)


    def stage(work):
        pl.when(me_head >= 0)(work)

    sent = []

    def send(src, dst, send_sem, recv_sem, device):
        copy = pltpu.make_async_remote_copy(
            src_ref=src, dst_ref=dst, send_sem=send_sem, recv_sem=recv_sem, device_id=device, device_id_type=MESH)
        copy.start()
        sent.append(copy)

    def arrived(dst, send_sem, recv_sem):
        pltpu.make_async_remote_copy(
            src_ref=dst, dst_ref=dst, send_sem=send_sem, recv_sem=recv_sem,
            device_id=(me_ctx, head_partner(1)), device_id_type=MESH).wait_recv()

    low, high = pl.ds(0, 64), pl.ds(64, 64)
    to_up, to_down = (me_ctx, up * 2 + core), (me_ctx, down * 2 + core)
    h_up, h_down, h_far = up * 2 + core, down * 2 + core, far * 2 + core
    s_up, s_down, s_far = up * 2 + 1 - core, down * 2 + 1 - core, far * 2 + 1 - core

    send(tok_ref.at[low], xall.at[me_head, low], gs.at[1], gr.at[1], to_up)
    send(tok_ref.at[high], xall.at[me_head, high], gs.at[2], gr.at[2], to_down)
    send(tok_ref, xall.at[me_head], gs.at[0], gr.at[0], sib)
    send(tok_ref.at[high], xall.at[me_head, high], gs.at[3], gr.at[3], to_up)
    send(tok_ref.at[low], xall.at[me_head, low], gs.at[4], gr.at[4], to_down)

    def pass_on(row, half, slot, device):
        send(xall.at[row, half], xall.at[row, half], gs.at[slot], gr.at[slot], device)

    def have(row, half, slot):
        arrived(xall.at[row, half], gs.at[slot], gr.at[slot])

    def project(group, first=False, then=None):
        def rows():
            return xall[pl.ds(2 * group, 2)].reshape(GROUP, DEPTH)

        @stage
        def _():
            made = jnp.dot(rows(), w_v[0], preferred_element_type=F32).astype(BF16).astype(F32)
            for h in range(2):
                kv_v[h] = made[:, 128 * h:128 * h + 128]

        for h in range(2):
            @stage
            def _():
                pair = kv_v[h]
                twice = doubled(pair, 0)

                def store(m, value):
                    phik[:, 128 * m:128 * m + 128] = value

                write_features(twice, store)
                values = pair.T[WIDTH:].astype(BF16)
                update = jnp.dot(values, phik[...], preferred_element_type=F32)
                if first:
                    state[h] = update
                else:
                    state[h] += update

            if then is not None:
                then(h)

        @stage
        def _():
            for h in range(2):
                pair = kv_v[h]
                kz_v[h, group] = jnp.where(lanes(GROUP) < WIDTH, pair, 0.0).astype(BF16)
                vk_v[h, group] = pltpu.roll(pair, WIDTH, 1).astype(BF16)
            made = jnp.dot(rows(), w_v[1], preferred_element_type=F32).astype(BF16)
            for h in range(2):
                q_v[h, group] = made[:, 128 * h:128 * h + 128]

    own.wait()
    for part in weights:
        part.wait()
    arrived(xall.at[me_head], gs.at[0], gr.at[0])
    project(y, True)

    have(h_down, low, 1)
    pass_on(h_down, low, 5, to_up)
    pass_on(h_down, low, 7, sib)
    have(h_up, high, 2)
    pass_on(h_up, high, 6, to_down)
    pass_on(h_up, high, 8, sib)

    context.wait()
    for at in range(0, PAIRS, 128):
        end = min(at + 128, PAIRS)
        ctx_f[at:end] = ctx_v[:, at:end].T
    start = 0
    for i in range(WIDTH):
        count = min(40, WIDTH - i)
        square[129 * i:129 * i + count] = ctx_f[start:start + count]
        start += WIDTH - i
    start = 0
    for i in range(WIDTH // 2):
        count = WIDTH // 2 - i
        square[pl.ds(128 * (i + 32) + 64 + i, count, 128)] = ctx_f[start + 32:start + 32 + count]
        start += WIDTH - i
    for apart in range(33):
        rows = square[pl.ds(apart, WIDTH, 129)]
        if apart == 0:
            ctx_f[2048:2112] = rows
            ctx_f[2112:2176] = jnp.zeros_like(rows)
        elif apart > 16:
            ctx_f[128 * (apart - 17):128 * (apart - 17) + 64] = rows
        else:
            at = 128 * (apart - 1) + 64
            ctx_f[at:at + 48] = rows[16:]
            ctx_f[at + 48:at + 64] = rows[:16]
    feature = lax.broadcasted_iota(jnp.int32, (1, FEAT), 1)
    in_second = (feature % 128) >= WIDTH
    diagonal = (feature >= 2048) & (feature < 2112)
    unused = feature >= 2112
    twin = (feature >= 15 * 128) & (feature < 15 * 128 + 64)
    square_weight = jnp.where(unused, 0.0, jnp.where(diagonal | twin, 1.0 / 64, 2.0 / 64)).astype(F32)
    single_weight = jnp.where(
        unused, 0.0, jnp.where(diagonal, 1.0 / 8, jnp.where(twin, math.sqrt(2.0) / 16, math.sqrt(2.0) / 8))).astype(F32)
    for m in range(CHUNKS):
        rows = ctx_f[128 * m:128 * m + 128].T
        ctx_t[:, :, 128 * m:128 * m + 128] = rows.reshape(8, 16, 128)

    have(h_down, high, 3)
    pass_on(h_down, high, 9, sib)
    have(h_up, low, 4)
    pass_on(h_up, low, 10, sib)
    have(s_down, low, 7)
    have(s_down, high, 9)
    project(down)
    have(s_up, high, 8)
    have(s_up, low, 10)
    project(up)
    have(h_far, low, 5)
    pass_on(h_far, low, 11, sib)
    have(h_far, high, 6)
    pass_on(h_far, high, 12, sib)
    have(s_far, low, 11)
    have(s_far, high, 12)

    def x_out(h):
        xs[h] = state[h].reshape(NX, 16, FEAT).astype(BF16)
        xr[h, x] = xs[h, x]
        for k in range(1, NX):
            there = (x + k) % NX
            send(xs.at[h, there], xr.at[h, x], xs_sem.at[h, k], xr_sem.at[h, k], (z * NX + there, me_head))

    def x_in(h):
        for k in range(1, NX):
            arrived(xr.at[h, (x + NX - k) % NX], xs_sem.at[h, k], xr_sem.at[h, k])
        total = xr[h, 0].astype(F32)
        for k in range(1, NX):
            total += xr[h, k].astype(F32)
        total = total.astype(BF16)
        for k in range(NZ):
            zs[h, k] = jnp.concatenate([total[:, 256 * k:256 * k + 256], total[:, 2048:]], axis=1)
        zr[h, z] = zs[h, z]
        for k in range(1, NZ):
            there = (z + k) % NZ
            send(zs.at[h, there], zr.at[h, z], zs_sem.at[h, k], zr_sem.at[h, k], (there * NX + x, me_head))

    def z_in(h):
        for k in range(1, NZ):
            arrived(zr.at[h, (z + NZ - k) % NZ], zs_sem.at[h, k], zr_sem.at[h, k])
        running = jnp.zeros((16, 256), F32)
        tail = jnp.zeros((16, 128), F32)
        for k in range(NZ):
            es[h, k] = running.astype(BF16)
            running += zr[h, k, :, :256].astype(F32)
            tail += jnp.where(k < z, zr[h, k, :, 256:].astype(F32), 0.0)
        tails[h] = tail
        er[h, z] = es[h, z]
        for k in range(1, NZ):
            there = (z + k) % NZ
            send(es.at[h, there], er.at[h, z], es_sem.at[h, k], er_sem.at[h, k], (there * NX + x, me_head))

    def e_in(h):
        for k in range(1, NZ):
            arrived(er.at[h, (z + NZ - k) % NZ], es_sem.at[h, k], er_sem.at[h, k])
        earlier = jnp.concatenate(
            [er[h, k].astype(F32) for k in range(NZ)] + [tails[h]], axis=1)
        before = ctx_t[4 * h + x] * single_weight
        running = earlier
        for k in range(NX):
            ps[h, k] = (before + running * square_weight).astype(BF16)
            if k < NX - 1:
                running += xr[h, k].astype(F32)
        pt[h, x] = ps[h, x]
        for k in range(1, NX):
            there = (x + k) % NX
            send(ps.at[h, there], pt.at[h, x], ps_sem.at[h, k], pr_sem.at[h, k], (z * NX + there, me_head))

    causal = (lax.broadcasted_iota(jnp.int32, (GROUP, GROUP), 1)
              <= lax.broadcasted_iota(jnp.int32, (GROUP, GROUP), 0))

    def tile(h, i):
        pair = q_v[h, i].astype(F32)
        for g in range(2):
            twice = doubled(pair, g)

            def store(m, value):
                phiq[h, i, g, :, 128 * m:128 * m + 128] = value

            write_features(twice, store)
            query = twice.astype(BF16)
            total = None
            for j in range(i + 1):
                score = lax.dot_general(
                    query, kz_v[h, j], (((1,), (1,)), ((), ())), preferred_element_type=F32)
                score = score * score * (1.0 / WIDTH)
                if j == i:
                    score = jnp.where(causal, score, 0.0)
                part = jnp.dot(score.astype(BF16), vk_v[h, j], preferred_element_type=F32)
                total = part if total is None else total + part
            comb[h, i, g] = total

    kept = []

    def finish(h):
        for k in range(1, NX):
            arrived(pt.at[h, (x + NX - k) % NX], ps_sem.at[h, k], pr_sem.at[h, k])
        turned[h] = pt[h].reshape(WIDTH, FEAT).astype(F32).T.astype(BF16)
        for k in (2, 1, 3, 0):
            i = (y + k) % NY

            @stage
            def _():
                carried = jnp.dot(
                    phiq[h, i].reshape(2 * GROUP, FEAT), turned[h], preferred_element_type=F32)
                combined = carried + comb[h, i].reshape(2 * GROUP, 128)[:, :WIDTH]
                inverse = lax.rsqrt(jnp.mean(combined * combined, -1, keepdims=True) + 1e-05)
                made = combined * inverse
                both = jnp.concatenate([made[:GROUP], made[GROUP:]], axis=1) * gain_ref[:, 128 * h:128 * h + 128]
                ob[h, pl.ds(2 * i, 2)] = both.astype(BF16).reshape(2, 128, 128)

            for d in range(2):
                there = i * 2 + (core + d) % 2
                if k == 0 and d == 0:
                    copy = pltpu.make_async_copy(ob.at[h, there], out_ref.at[2 * me_head + h], local_sem.at[3 + h])
                    copy.start()
                    kept.append(copy)
                else:
                    send(ob.at[h, there], out_ref.at[2 * me_head + h],
                         os_sem.at[h, 2 * k + d], or_sem.at[h, 2 * k + d], (me_ctx, there))

    @pl.when(core == 1)
    def _():
        pl.semaphore_wait(barrier, 2 * (NX - 1 + NZ - 1))
        pl.semaphore_signal(met.at[1], inc=1, device_id=sib, device_id_type=MESH)

    @pl.when(core == 0)
    def _():
        pl.semaphore_wait(met.at[1], 1)

    project(far, then=x_out)
    stage(functools.partial(tile, 0, 0))
    stage(functools.partial(tile, 0, 1))
    stage(functools.partial(tile, 0, 2))
    x_in(0)
    stage(functools.partial(tile, 0, 3))
    x_in(1)
    stage(functools.partial(tile, 1, 0))
    stage(functools.partial(tile, 1, 1))
    z_in(0)
    stage(functools.partial(tile, 1, 2))
    z_in(1)
    stage(functools.partial(tile, 1, 3))
    e_in(0)
    e_in(1)
    finish(0)
    finish(1)
    for copy in kept:
        copy.wait()
    for h in range(2):
        for k in range(NY):
            for d in range(2):
                if k + d > 0:
                    there = ((y + NY - k) % NY) * 2 + (core + d) % 2
                    arrived(out_ref.at[2 * there + h], os_sem.at[h, 2 * k + d], or_sem.at[h, 2 * k + d])
    for copy in sent:
        copy.wait_send()


def local(tokens, projection, context_state, norm_gain):
    dma = pltpu.SemaphoreType.DMA
    pieces = pl.pallas_call(
        kernel,
        out_shape=jax.ShapeDtypeStruct((4 * NY, 128, 128), BF16),
        in_specs=[pl.BlockSpec(memory_space=pl.ANY)] * 3 + [pl.BlockSpec(memory_space=pltpu.VMEM)],
        out_specs=pl.BlockSpec(memory_space=pl.ANY),
        scratch_shapes=[
            pltpu.VMEM((2, DEPTH, 256), BF16),
            pltpu.VMEM((128, PAIRS), F32),
            pltpu.VMEM((2 * NY, 128, DEPTH), BF16),
            pltpu.VMEM((2, 4, GROUP, 128), BF16),
            pltpu.VMEM((2, 4, GROUP, 128), BF16),
            pltpu.VMEM((2, 4, GROUP, 128), BF16),
            pltpu.VMEM((2, GROUP, 128), F32),
            pltpu.VMEM((GROUP, FEAT), BF16),
            pltpu.VMEM((2, WIDTH, FEAT), F32),
            pltpu.VMEM((2, 4, 2, GROUP, FEAT), BF16),
            pltpu.VMEM((2, 4, 2, GROUP, 128), F32),
            pltpu.VMEM((64 * 129 + 8, 128), F32),
            pltpu.VMEM((FEAT, 128), F32),
            pltpu.VMEM((8, 16, FEAT), F32),
            pltpu.VMEM((2, NX, 16, FEAT), BF16),
            pltpu.VMEM((2, NX, 16, FEAT), BF16),
            pltpu.VMEM((2, NZ, 16, PIECE), BF16),
            pltpu.VMEM((2, NZ, 16, PIECE), BF16),
            pltpu.VMEM((2, NZ, 16, 256), BF16),
            pltpu.VMEM((2, NZ, 16, 256), BF16),
            pltpu.VMEM((2, 16, 128), F32),
            pltpu.VMEM((2, NX, 16, FEAT), BF16),
            pltpu.VMEM((2, NX, 16, FEAT), BF16),
            pltpu.VMEM((2, FEAT, WIDTH), BF16),
            pltpu.VMEM((2, 2 * NY, 128, 128), BF16),
            pltpu.SemaphoreType.REGULAR((2,)),
            dma((9,)),
            dma((13,)),
            dma((13,)),
            dma((2, NX)),
            dma((2, NX)),
            dma((2, NZ)),
            dma((2, NZ)),
            dma((2, NZ)),
            dma((2, NZ)),
            dma((2, NX)),
            dma((2, NX)),
            dma((2, 2 * NY)),
            dma((2, 2 * NY)),
        ],
        compiler_params=pltpu.CompilerParams(
            collective_id=0, has_side_effects=True, vmem_limit_bytes=58 * 2**20),
        cost_estimate=pl.CostEstimate(flops=10 * 10**9, bytes_accessed=8 * 2**20, transcendentals=0),
    )(tokens, projection, jnp.swapaxes(context_state, 1, 2).reshape(128, PAIRS), norm_gain.reshape(1, -1))
    return jnp.swapaxes(pieces, 0, 1).reshape(128, 2048)


def solution(mesh):
    placed = (P(("ctx", "head"), None), P(None, "head"), P("head", None, None), P("head"))
    return jax.shard_map(
        local, mesh=mesh, in_specs=placed, out_specs=P(("ctx", "head"), None), check_vma=False
    )
```

```python
import functools
import math

import jax
import jax.numpy as jnp
from jax import lax
from jax.experimental import pallas as pl
from jax.experimental.pallas import tpu as pltpu
from jax.sharding import PartitionSpec as P

MESH = pl.DeviceIdType.MESH
NZ, NX, NY = 8, 4, 4
WIDTH = 64
TOKENS = 1024
GROUP = 256
DEPTH = 2048
CHUNKS = 17
FEAT = 128 * CHUNKS
PARTS = ((0, 1024), (1024, FEAT))
PAIRS = 2080
FAR_FIRST_X, FAR_FIRST_Z = (2, 1, 3), (4, 3, 5, 2, 6, 1, 7)
F32, BF16 = jnp.float32, jnp.bfloat16


def lanes(rows):
    return lax.broadcasted_iota(jnp.int32, (rows, 128), 1)


def left(value, amount):
    return pltpu.roll(value, 128 - amount, 1)


def write_features(twice, store, chunks=range(17)):
    base = jnp.where(lanes(twice.shape[0]) < WIDTH, twice, left(twice, 16))
    for m in chunks:
        store(m, (base * left(twice, 17 + m) if m < 16 else twice * twice).astype(BF16))


def doubled(pair, half):
    low = lanes(pair.shape[0]) < WIDTH
    turned = pltpu.roll(pair, WIDTH, 1)
    return jnp.where(low, pair, turned) if half == 0 else jnp.where(low, turned, pair)


def kernel(tok_ref, w_hbm, ctx_hbm, gain_ref, out_ref,
           w_v, ctx_v, xall, q_v, kz_v, vk_v, kv_v, phik, state, phiq, comb,
           square, ctx_f, ctx_t, xs, xr, zs, zr, es, er, tails, ps, pt, turned, ob,
           met, local_sem, gs, gr, xs_sem, xr_sem, zs_sem, zr_sem, es_sem, er_sem, ps_sem, pr_sem, os_sem, or_sem):
    me_ctx, me_head = lax.axis_index("ctx"), lax.axis_index("head")
    z, x = me_ctx // NX, me_ctx % NX
    y, core = me_head // 2, me_head % 2
    up, down, far = (y + 1) % NY, (y + NY - 1) % NY, (y + 2) % NY

    def head_partner(k):
        return (me_head + k) % (2 * NY)

    barrier = pltpu.get_barrier_semaphore()
    sib = (me_ctx, y * 2 + 1 - core)
    for other in (up, down):
        pl.semaphore_signal(barrier, inc=1, device_id=(me_ctx, other * 2), device_id_type=MESH)

    @pl.when(core == 1)
    def _():
        pl.semaphore_signal(barrier, inc=1, device_id=sib, device_id_type=MESH)

    for k in range(1, NX):
        pl.semaphore_signal(barrier, inc=1, device_id=(z * NX + (x + k) % NX, y * 2 + 1), device_id_type=MESH)
    for k in range(1, NZ):
        pl.semaphore_signal(barrier, inc=1, device_id=(((z + k) % NZ) * NX + x, y * 2 + 1), device_id_type=MESH)

    own = pltpu.make_async_copy(tok_ref, xall.at[me_head], local_sem.at[0])
    weights = []
    for n, at in enumerate((128, 384, 0, 256)):
        weights.append(pltpu.make_async_copy(
            w_hbm.at[:, at:at + 128], w_v.at[n // 2, :, 128 * (n % 2):128 * (n % 2) + 128], local_sem.at[5 + n]))
    context = pltpu.make_async_copy(ctx_hbm, ctx_v, local_sem.at[2])
    own.start()
    for part in weights:
        part.start()
    context.start()

    @pl.when(core == 0)
    def _():
        pl.semaphore_wait(barrier, 5)
        pl.semaphore_signal(met.at[0], inc=1, device_id=sib, device_id_type=MESH)

    @pl.when(core == 1)
    def _():
        pl.semaphore_wait(met.at[0], 1)


    def stage(work):
        pl.when(me_head >= 0)(work)

    sent = []

    def send(src, dst, send_sem, recv_sem, device):
        copy = pltpu.make_async_remote_copy(
            src_ref=src, dst_ref=dst, send_sem=send_sem, recv_sem=recv_sem, device_id=device, device_id_type=MESH)
        copy.start()
        sent.append(copy)

    def arrived(dst, send_sem, recv_sem):
        pltpu.make_async_remote_copy(
            src_ref=dst, dst_ref=dst, send_sem=send_sem, recv_sem=recv_sem,
            device_id=(me_ctx, head_partner(1)), device_id_type=MESH).wait_recv()

    low, high = pl.ds(0, 64), pl.ds(64, 64)
    to_up, to_down = (me_ctx, up * 2 + core), (me_ctx, down * 2 + core)
    h_up, h_down, h_far = up * 2 + core, down * 2 + core, far * 2 + core
    s_up, s_down, s_far = up * 2 + 1 - core, down * 2 + 1 - core, far * 2 + 1 - core

    send(tok_ref.at[low], xall.at[me_head, low], gs.at[1], gr.at[1], to_up)
    send(tok_ref.at[high], xall.at[me_head, high], gs.at[2], gr.at[2], to_down)
    send(tok_ref, xall.at[me_head], gs.at[0], gr.at[0], sib)
    send(tok_ref.at[high], xall.at[me_head, high], gs.at[3], gr.at[3], to_up)
    send(tok_ref.at[low], xall.at[me_head, low], gs.at[4], gr.at[4], to_down)

    def pass_on(row, half, slot, device):
        send(xall.at[row, half], xall.at[row, half], gs.at[slot], gr.at[slot], device)

    def have(row, half, slot):
        arrived(xall.at[row, half], gs.at[slot], gr.at[slot])

    def span(half):
        return pl.ds(half * 128, 128) if isinstance(half, int) else pl.ds(pl.multiple_of(half * 128, 128), 128)

    def project(group, first=False, then=None, rest=None):
        def rows():
            return xall[pl.ds(2 * group, 2)].reshape(GROUP, DEPTH)

        def key_values(half):
            block = xall[2 * group + half]
            made = jnp.dot(block, w_v[0], preferred_element_type=F32).astype(BF16).astype(F32)
            for h in range(2):
                kv_v[h, span(half)] = made[:, 128 * h:128 * h + 128]

        def expand(h, half):
            def store(m, value):
                phik[h, span(half), 128 * m:128 * m + 128] = value

            write_features(doubled(kv_v[h, span(half)], 0), store)

        def add(h, part):
            lo, hi = PARTS[part]
            values = kv_v[h].T[WIDTH:].astype(BF16)
            update = jnp.dot(values, phik[h, :, lo:hi], preferred_element_type=F32)
            if first:
                state[h, :, lo:hi] = update
            else:
                state[h, :, lo:hi] += update

        if then is None:
            @stage
            def _():
                made = jnp.dot(rows(), w_v[0], preferred_element_type=F32).astype(BF16).astype(F32)
                for h in range(2):
                    kv_v[h] = made[:, 128 * h:128 * h + 128]
                    for half in range(2):
                        expand(h, half)
                    add(h, 0)
                    add(h, 1)
        else:
            @stage
            def _():
                key_values(core)
                expand(0, core)
                expand(1, core)

            rest()

            @stage
            def _():
                key_values(1 - core)
                expand(0, 1 - core)
                add(0, 0)

            then(0, 0)

            @stage
            def _():
                add(0, 1)
                expand(1, 1 - core)

            then(0, 1)

            @stage
            def _():
                add(1, 0)

            then(1, 0)

            @stage
            def _():
                add(1, 1)

            then(1, 1)

        @stage
        def _():
            for h in range(2):
                pair = kv_v[h]
                kz_v[h, group] = jnp.where(lanes(GROUP) < WIDTH, pair, 0.0).astype(BF16)
                vk_v[h, group] = pltpu.roll(pair, WIDTH, 1).astype(BF16)
            made = jnp.dot(rows(), w_v[1], preferred_element_type=F32).astype(BF16)
            for h in range(2):
                q_v[h, group] = made[:, 128 * h:128 * h + 128]

    own.wait()
    for part in weights:
        part.wait()
    arrived(xall.at[me_head], gs.at[0], gr.at[0])
    project(y, True)

    have(h_down, low, 1)
    pass_on(h_down, low, 5, to_up)
    pass_on(h_down, low, 7, sib)
    have(h_up, high, 2)
    pass_on(h_up, high, 6, to_down)
    pass_on(h_up, high, 8, sib)

    context.wait()
    for at in range(0, PAIRS, 128):
        end = min(at + 128, PAIRS)
        ctx_f[at:end] = ctx_v[:, at:end].T
    start = 0
    for i in range(WIDTH):
        count = min(40, WIDTH - i)
        square[129 * i:129 * i + count] = ctx_f[start:start + count]
        start += WIDTH - i
    start = 0
    for i in range(WIDTH // 2):
        count = WIDTH // 2 - i
        square[pl.ds(128 * (i + 32) + 64 + i, count, 128)] = ctx_f[start + 32:start + 32 + count]
        start += WIDTH - i
    for apart in range(33):
        rows = square[pl.ds(apart, WIDTH, 129)]
        if apart == 0:
            ctx_f[2048:2112] = rows
            ctx_f[2112:2176] = jnp.zeros_like(rows)
        elif apart > 16:
            ctx_f[128 * (apart - 17):128 * (apart - 17) + 64] = rows
        else:
            at = 128 * (apart - 1) + 64
            ctx_f[at:at + 48] = rows[16:]
            ctx_f[at + 48:at + 64] = rows[:16]
    feature = lax.broadcasted_iota(jnp.int32, (1, FEAT), 1)
    in_second = (feature % 128) >= WIDTH
    diagonal = (feature >= 2048) & (feature < 2112)
    unused = feature >= 2112
    twin = (feature >= 15 * 128) & (feature < 15 * 128 + 64)
    square_weight = jnp.where(unused, 0.0, jnp.where(diagonal | twin, 1.0 / 64, 2.0 / 64)).astype(F32)
    single_weight = jnp.where(
        unused, 0.0, jnp.where(diagonal, 1.0 / 8, jnp.where(twin, math.sqrt(2.0) / 16, math.sqrt(2.0) / 8))).astype(F32)
    for m in range(CHUNKS):
        rows = ctx_f[128 * m:128 * m + 128].T
        ctx_t[:, :, 128 * m:128 * m + 128] = rows.reshape(8, 16, 128)

    have(h_down, high, 3)
    pass_on(h_down, high, 9, sib)
    have(h_up, low, 4)
    pass_on(h_up, low, 10, sib)
    have(s_down, low, 7)
    have(s_down, high, 9)
    project(down)
    have(s_up, high, 8)
    have(s_up, low, 10)
    project(up)
    @pl.when(core == 1)
    def _():
        pl.semaphore_wait(barrier, 2 * (NX - 1 + NZ - 1))
        pl.semaphore_signal(met.at[1], inc=1, device_id=sib, device_id_type=MESH)

    @pl.when(core == 0)
    def _():
        pl.semaphore_wait(met.at[1], 1)

    have(h_far, low, 5)
    pass_on(h_far, low, 11, sib)
    have(h_far, high, 6)
    pass_on(h_far, high, 12, sib)

    def x_out(h, part):
        lo, hi = PARTS[part]
        c = 2 * h + part
        xs[part][h] = state[h, :, lo:hi].reshape(NX, 16, hi - lo).astype(BF16)
        xr[part][h, x] = xs[part][h, x]
        for k in FAR_FIRST_X:
            there = (x + k) % NX
            send(xs[part].at[h, there], xr[part].at[h, x], xs_sem.at[c, k], xr_sem.at[c, k], (z * NX + there, me_head))

    def x_in(h, part):
        c = 2 * h + part
        for k in range(1, NX):
            arrived(xr[part].at[h, (x + NX - k) % NX], xs_sem.at[c, k], xr_sem.at[c, k])
        total = xr[part][h, 0].astype(F32)
        for k in range(1, NX):
            total += xr[part][h, k].astype(F32)
        total = total.astype(BF16)
        for k in range(NZ):
            piece = total[:, 128 * k:128 * k + 128]
            zs[part][h, k] = piece if part == 0 else jnp.concatenate([piece, total[:, 1024:]], axis=1)
        zr[part][h, z] = zs[part][h, z]
        for k in FAR_FIRST_Z:
            there = (z + k) % NZ
            send(zs[part].at[h, there], zr[part].at[h, z], zs_sem.at[c, k], zr_sem.at[c, k], (there * NX + x, me_head))

    def z_in(h, part):
        c = 2 * h + part
        for k in range(1, NZ):
            arrived(zr[part].at[h, (z + NZ - k) % NZ], zs_sem.at[c, k], zr_sem.at[c, k])
        running = jnp.zeros((16, 128), F32)
        tail = jnp.zeros((16, 128), F32)
        for k in range(NZ):
            es[part][h, k] = running.astype(BF16)
            running += zr[part][h, k, :, :128].astype(F32)
            if part == 1:
                tail += jnp.where(k < z, zr[part][h, k, :, 128:].astype(F32), 0.0)
        if part == 1:
            tails[h] = tail
        er[part][h, z] = es[part][h, z]
        for k in FAR_FIRST_Z:
            there = (z + k) % NZ
            send(es[part].at[h, there], er[part].at[h, z], es_sem.at[c, k], er_sem.at[c, k], (there * NX + x, me_head))

    def e_in(h, part):
        lo, hi = PARTS[part]
        c = 2 * h + part
        for k in range(1, NZ):
            arrived(er[part].at[h, (z + NZ - k) % NZ], es_sem.at[c, k], er_sem.at[c, k])
        running = jnp.concatenate(
            [er[part][h, k].astype(F32) for k in range(NZ)] + ([tails[h]] if part == 1 else []), axis=1)
        before = ctx_t[4 * h + x, :, lo:hi] * single_weight[:, lo:hi]
        for k in range(NX):
            ps[part][h, k] = (before + running * square_weight[:, lo:hi]).astype(BF16)
            if k < NX - 1:
                running += xr[part][h, k].astype(F32)
        pt[part][h, x] = ps[part][h, x]
        for k in FAR_FIRST_X:
            there = (x + k) % NX
            send(ps[part].at[h, there], pt[part].at[h, x], ps_sem.at[c, k], pr_sem.at[c, k], (z * NX + there, me_head))

    causal = (lax.broadcasted_iota(jnp.int32, (GROUP, GROUP), 1)
              <= lax.broadcasted_iota(jnp.int32, (GROUP, GROUP), 0))

    def tile(h, i):
        pair = q_v[h, i].astype(F32)
        for g in range(2):
            twice = doubled(pair, g)

            def store(m, value):
                phiq[h, i, g, :, 128 * m:128 * m + 128] = value

            write_features(twice, store)
            query = twice.astype(BF16)
            total = None
            for j in range(i + 1):
                score = lax.dot_general(
                    query, kz_v[h, j], (((1,), (1,)), ((), ())), preferred_element_type=F32)
                score = score * score * (1.0 / WIDTH)
                if j == i:
                    score = jnp.where(causal, score, 0.0)
                part = jnp.dot(score.astype(BF16), vk_v[h, j], preferred_element_type=F32)
                total = part if total is None else total + part
            comb[h, i, g] = total

    kept = []

    def finish(h, part):
        lo, hi = PARTS[part]
        c = 2 * h + part
        for k in range(1, NX):
            arrived(pt[part].at[h, (x + NX - k) % NX], ps_sem.at[c, k], pr_sem.at[c, k])
        turned[h, lo:hi] = pt[part][h].reshape(WIDTH, hi - lo).astype(F32).T.astype(BF16)
        for k in (2, 1, 3, 0):
            i = (y + k) % NY

            @stage
            def _():
                carried = jnp.dot(
                    phiq[h, i, :, :, lo:hi].reshape(2 * GROUP, hi - lo), turned[h, lo:hi], preferred_element_type=F32)
                combined = carried + comb[h, i].reshape(2 * GROUP, 128)[:, :WIDTH]
                if part == 0:
                    comb[h, i, :, :, :WIDTH] = combined.reshape(2, GROUP, WIDTH)
                    return
                inverse = lax.rsqrt(jnp.mean(combined * combined, -1, keepdims=True) + 1e-05)
                made = combined * inverse
                both = jnp.concatenate([made[:GROUP], made[GROUP:]], axis=1) * gain_ref[:, 128 * h:128 * h + 128]
                ob[h, pl.ds(2 * i, 2)] = both.astype(BF16).reshape(2, 128, 128)

            if part == 0:
                continue
            for d in range(2):
                there = i * 2 + (core + d) % 2
                if k == 0 and d == 0:
                    copy = pltpu.make_async_copy(ob.at[h, there], out_ref.at[2 * me_head + h], local_sem.at[3 + h])
                    copy.start()
                    kept.append(copy)
                else:
                    send(ob.at[h, there], out_ref.at[2 * me_head + h],
                         os_sem.at[h, 2 * k + d], or_sem.at[h, 2 * k + d], (me_ctx, there))

    def rest():
        have(s_far, low, 11)
        have(s_far, high, 12)

    project(far, then=x_out, rest=rest)
    order = [(h, part) for h in range(2) for part in range(2)]
    tiles = [(h, i) for h in range(2) for i in range(4)]
    for step, counts in ((x_in, (2, 1, 1, 1)), (z_in, (1, 1, 1, 0))):
        for now, count in zip(order, counts):
            for _ in range(count):
                stage(functools.partial(tile, *tiles.pop(0)))
            step(*now)
    for now in order:
        e_in(*now)
    for now in order:
        finish(*now)
    for copy in kept:
        copy.wait()
    for h in range(2):
        for k in range(NY):
            for d in range(2):
                if k + d > 0:
                    there = ((y + NY - k) % NY) * 2 + (core + d) % 2
                    arrived(out_ref.at[2 * there + h], os_sem.at[h, 2 * k + d], or_sem.at[h, 2 * k + d])
    for copy in sent:
        copy.wait_send()


def local(tokens, projection, context_state, norm_gain):
    dma = pltpu.SemaphoreType.DMA

    def parted(count, *widths):
        return [pltpu.VMEM((2, count, 16, width), BF16) for width in widths]

    pieces = pl.pallas_call(
        kernel,
        out_shape=jax.ShapeDtypeStruct((4 * NY, 128, 128), BF16),
        in_specs=[pl.BlockSpec(memory_space=pl.ANY)] * 3 + [pl.BlockSpec(memory_space=pltpu.VMEM)],
        out_specs=pl.BlockSpec(memory_space=pl.ANY),
        scratch_shapes=[
            pltpu.VMEM((2, DEPTH, 256), BF16),
            pltpu.VMEM((128, PAIRS), F32),
            pltpu.VMEM((2 * NY, 128, DEPTH), BF16),
            pltpu.VMEM((2, 4, GROUP, 128), BF16),
            pltpu.VMEM((2, 4, GROUP, 128), BF16),
            pltpu.VMEM((2, 4, GROUP, 128), BF16),
            pltpu.VMEM((2, GROUP, 128), F32),
            pltpu.VMEM((2, GROUP, FEAT), BF16),
            pltpu.VMEM((2, WIDTH, FEAT), F32),
            pltpu.VMEM((2, 4, 2, GROUP, FEAT), BF16),
            pltpu.VMEM((2, 4, 2, GROUP, 128), F32),
            pltpu.VMEM((64 * 129 + 8, 128), F32),
            pltpu.VMEM((FEAT, 128), F32),
            pltpu.VMEM((8, 16, FEAT), F32),
            parted(NX, 1024, 1152),
            parted(NX, 1024, 1152),
            parted(NZ, 128, 256),
            parted(NZ, 128, 256),
            parted(NZ, 128, 128),
            parted(NZ, 128, 128),
            pltpu.VMEM((2, 16, 128), F32),
            parted(NX, 1024, 1152),
            parted(NX, 1024, 1152),
            pltpu.VMEM((2, FEAT, WIDTH), BF16),
            pltpu.VMEM((2, 2 * NY, 128, 128), BF16),
            pltpu.SemaphoreType.REGULAR((2,)),
            dma((9,)),
            dma((13,)),
            dma((13,)),
            dma((4, NX)),
            dma((4, NX)),
            dma((4, NZ)),
            dma((4, NZ)),
            dma((4, NZ)),
            dma((4, NZ)),
            dma((4, NX)),
            dma((4, NX)),
            dma((2, 2 * NY)),
            dma((2, 2 * NY)),
        ],
        compiler_params=pltpu.CompilerParams(
            collective_id=0, has_side_effects=True, vmem_limit_bytes=58 * 2**20),
        cost_estimate=pl.CostEstimate(flops=10 * 10**9, bytes_accessed=8 * 2**20, transcendentals=0),
    )(tokens, projection, jnp.swapaxes(context_state, 1, 2).reshape(128, PAIRS), norm_gain.reshape(1, -1))
    return jnp.swapaxes(pieces, 0, 1).reshape(128, 2048)


def solution(mesh):
    placed = (P(("ctx", "head"), None), P(None, "head"), P("head", None, None), P("head"))
    return jax.shard_map(
        local, mesh=mesh, in_specs=placed, out_specs=P(("ctx", "head"), None), check_vma=False
    )
```
